128 devices in a mesh: chan: 8 (over z, y_lo), win: 16 (over y_hi, x, core).
Axes of the slice: x: 4, y: 4 (y_hi: 2, y_lo: 2; y = y_hi * 2 + y_lo), z: 4, core: 2. Of those that a mesh axis runs over, the one named last changes fastest.
Arguments:
- raw_traces: bfloat16 [32, 2048, 4096], P('win', None, 'chan'), may hold values from -6 to 6
- fir_taps: bfloat16 [32], replicated, may hold values from -1 to 1
- source_ids: int32 [4], replicated, may hold values from 0 to 15
- window_offsets: int32 [32], P('win'), may hold values from 0 to 3
Outputs:
- correlations: float32 [16384, 2048], P('win', 'chan')
The draws below stay inside these ranges and needn't reach their ends.
All inputs are finite; a program needn't handle non-finite values.
Results may differ from the reference program's by a relative error of at most 0.008.
Values may be sent and summed in bfloat16 or wider, within the bound.
No kernel may reach another device: no remote copies, remote signals or barrier semaphores. Data moves between devices by JAX's collectives and lax.ppermute only.
A program may use at most 192 MiB of HBM per device.

```python
import math
import jax
import jax.numpy as jnp
from jax import lax

CHANNELS = 2048
BLOCK = 128
SAMPLES = 4096
DECIM = 4
TAPS = 32
BAND = 64
NSRC = 4
LAGS = 32
WINDOWS = 32
FREQS = 512
BLOCKS = 16


def set_ends(values, own_key, least, high):
    longest = values.shape.index(max(values.shape))
    spots = []
    for shift in (0, 1):
        where = [jax.random.randint(jax.random.fold_in(own_key, axis), (), 0, length) for axis, length in enumerate(values.shape)]
        where[longest] = (where[longest] + shift) % values.shape[longest]
        spots.append(tuple(where))
    return values.at[spots[0]].set(least).at[spots[1]].set(high)


def levels(key, dims, shards, smallest, high):
    factor_of = 1.0
    for axis_at, parts in shards:
        heights = jax.random.uniform(jax.random.fold_in(jax.random.fold_in(key, 6), axis_at), (parts,), jnp.float32, smallest / len(shards), high / len(shards))
        factor_of = factor_of * jnp.repeat(jnp.exp(heights), dims[axis_at] // parts).reshape((-1,) + (1,) * (len(dims) - 1 - axis_at))
    return factor_of


def normal_values(own_key, dims, width, most, pieces=(), kind=jnp.bfloat16):
    gain = levels(own_key, dims, pieces, -0.22, 0.18) if pieces else 1.0
    entries = jax.random.normal(own_key, dims, jnp.float32) * width * gain
    return jnp.minimum(jnp.maximum(entries, -most), most).astype(kind)


def setup_inputs(seed: int = 0) -> dict:
    key_list = jax.random.split(jax.random.key(seed), 5)
    raw_traces = normal_values(key_list[0], (WINDOWS, CHANNELS, SAMPLES), 1.0, 6.0, ((0, 16), (2, 8)))
    fir_taps = normal_values(key_list[1], (TAPS,), TAPS ** -0.5, 1.0)
    source_ids = set_ends(jax.random.randint(key_list[2], (NSRC,), 0, BLOCKS), jax.random.fold_in(key_list[2], 1), 0, BLOCKS - 1).astype(jnp.int32)
    window_offsets = set_ends(jax.random.randint(key_list[3], (WINDOWS,), 0, DECIM), jax.random.fold_in(key_list[3], 1), 0, DECIM - 1).astype(jnp.int32)
    return dict(raw_traces=raw_traces, fir_taps=fir_taps, source_ids=source_ids, window_offsets=window_offsets)


epsilon = 1e-06
clip_level = 2.0

def decimate(normed, tap_values, offsets):
    windows_here, channels_here, samples = normed.shape
    tap_count = tap_values.shape[0]
    tile_len = 512 if samples % 512 == 0 else samples
    tile_count = samples // tile_len
    out_width = tile_len // DECIM
    tile_pos = jnp.arange(tile_len, dtype=jnp.int32)[:, None]
    out_pos = jnp.arange(out_width, dtype=jnp.int32)[None, :]
    base_shift = DECIM * out_pos - tile_pos
    distance = base_shift[None] + offsets.astype(jnp.int32)[:, None, None]
    tap_ids = jnp.arange(tap_count, dtype=jnp.int32)
    tap_float = tap_values.astype(jnp.float32)

    def banded(shift_amount):
        onehot = (distance[..., None] + shift_amount == tap_ids).astype(jnp.float32)
        return jnp.einsum('wtmk,k->wtm', onehot, tap_float).astype(jnp.bfloat16)
    own_matrix = banded(0)
    prior_matrix = banded(tile_len)
    tiles = normed.reshape(windows_here, channels_here, tile_count, tile_len)
    prior_tiles = jnp.concatenate([jnp.zeros_like(tiles[:, :, :1]), tiles[:, :, :-1]], axis=2)
    result = jnp.einsum('wcbt,wtm->wcbm', tiles.astype(jnp.float32), own_matrix.astype(jnp.float32))
    result = result + jnp.einsum('wcbt,wtm->wcbm', prior_tiles.astype(jnp.float32), prior_matrix.astype(jnp.float32))
    return result.reshape(windows_here, channels_here, tile_count * out_width).astype(jnp.bfloat16)

def transform_table(length):
    freq_count = length // 2
    sample_ids = jnp.arange(length, dtype=jnp.int32)[:, None]
    freq_ids = jnp.arange(freq_count, dtype=jnp.int32)[None, :]
    angles = (sample_ids * freq_ids % length).astype(jnp.float32) * (2.0 * math.pi / length)
    return jnp.concatenate([jnp.cos(angles), -jnp.sin(angles)], axis=1).astype(jnp.bfloat16)

def whiten_window(raw_block, tap_values, offsets):
    values = raw_block.astype(jnp.float32)
    mean_square = lax.optimization_barrier(jnp.mean(values * values, axis=-1, keepdims=True))
    normed = jnp.clip(values / jnp.sqrt(mean_square + epsilon), -clip_level, clip_level).astype(jnp.bfloat16)
    decimated = decimate(normed, tap_values, offsets)
    windows_here, channels_here, length = decimated.shape
    cos_sin = transform_table(length)
    transform = jnp.dot(decimated.reshape(windows_here * channels_here, length), cos_sin, preferred_element_type=jnp.float32)
    freq_count = length // 2
    halves = transform.reshape(windows_here, channels_here, 2, freq_count // BAND, BAND)
    energy = lax.optimization_barrier(jnp.mean(halves[:, :, 0] * halves[:, :, 0] + halves[:, :, 1] * halves[:, :, 1], axis=-1, keepdims=True))
    whitened = halves / jnp.sqrt(energy + epsilon)[:, :, None]
    return whitened.reshape(windows_here, channels_here, length).astype(jnp.bfloat16)

def modulate(source_rows, lag_count):
    window_count, row_count, length = source_rows.shape
    freq_count = length // 2
    lag_ids = jnp.arange(1, lag_count + 1, dtype=jnp.int32)[:, None]
    freq_ids = jnp.arange(freq_count, dtype=jnp.int32)[None, :]
    angles = (lag_ids * freq_ids % length).astype(jnp.float32) * (2.0 * math.pi / length)
    cos_part = jnp.cos(angles)
    sin_part = jnp.sin(angles)
    real_part = source_rows[..., :freq_count].astype(jnp.float32)[:, :, None, :]
    imag_part = source_rows[..., freq_count:].astype(jnp.float32)[:, :, None, :]
    mod_real = real_part * cos_part - imag_part * sin_part
    mod_imag = real_part * sin_part + imag_part * cos_part
    joined = jnp.concatenate([mod_real, mod_imag], axis=-1).astype(jnp.bfloat16)
    return joined.reshape(window_count, row_count * lag_count, length)

def reference(raw_traces, fir_taps, source_ids, window_offsets):

    def one_window(packed):
        raw_window, offset_one = packed
        return whiten_window(raw_window[None], fir_taps, offset_one[None])[0]
    spectra = lax.map(one_window, (raw_traces, window_offsets))
    chosen_blocks = []
    for source_step in range(NSRC):
        first_channel = (source_ids[source_step] * BLOCK).astype(jnp.int32)
        chosen_blocks.append(lax.dynamic_slice_in_dim(spectra, first_channel, BLOCK, 1))
    sources = jnp.concatenate(chosen_blocks, axis=1)

    def add_window(total, packed):
        sources_one, receivers_one = packed
        modulated = modulate(sources_one[None], LAGS)[0]
        return (total + jnp.dot(modulated.astype(jnp.float32), receivers_one.astype(jnp.float32).T), None)
    start_total = jnp.zeros((NSRC * BLOCK * LAGS, CHANNELS), jnp.float32)
    total = lax.scan(add_window, start_total, (sources, spectra))[0]
    return total / math.sqrt(FREQS * WINDOWS)
```

```python
import functools
import math

import jax
import jax.numpy as jnp
import numpy as np
from jax import lax
from jax.experimental import pallas as pl
from jax.experimental.pallas import tpu as pltpu
from jax.sharding import PartitionSpec as P

SAMPLES = 4096
DECIM = 4
TAPS = 32
NSRC = 4
LENGTH = 1024
FREQS = 512
BAND = 64
NCHAN = 8
NPAIR = 8
FINE = 8
COARSE = 4
STAGES = 2
HERE = 512
OUT = HERE // DECIM
RECV = 256
PART = 32 // STAGES
ROWS = NPAIR * PART
VMEM = 56 * 1024 * 1024

epsilon = 1e-06
clip_level = 2.0

f32 = jnp.float32
bf16 = jnp.bfloat16

NT = (((1,), (1,)), ((), ()))
TN = (((0,), (0,)), ((), ()))


def dot(a, b, dims=None):
    if dims is None:
        return jnp.dot(a, b, preferred_element_type=f32)
    return lax.dot_general(a, b, dims, preferred_element_type=f32)


def split_dot(left, sq, dims, flip=False):
    hi = sq.astype(bf16)
    lo = (sq - hi.astype(f32)).astype(bf16)
    if flip:
        return dot(hi, left, dims) + dot(lo, left, dims)
    return dot(left, hi, dims) + dot(left, lo, dims)


def params(limit=VMEM):
    return pltpu.CompilerParams(vmem_limit_bytes=limit)


def cost(flops, nbytes):
    return pl.CostEstimate(flops=int(flops), bytes_accessed=int(nbytes), transcendentals=0)


@functools.lru_cache(None)
def tables():
    m = np.arange(LENGTH)[:, None]
    f = np.arange(FREQS)[None, :]
    ang = (m * f % LENGTH).astype(np.float64) * (2.0 * math.pi / LENGTH)
    table = np.concatenate([np.cos(ang), -np.sin(ang)], axis=1).astype(jnp.bfloat16)
    band = np.kron(np.eye(FREQS // BAND), np.ones((BAND, BAND))) / BAND
    lag = np.arange(1, FINE + 1)[:, None]
    fine = (lag * f % LENGTH) * (2.0 * math.pi / LENGTH)
    fine = np.concatenate([np.cos(fine), np.sin(fine)], axis=1).astype(np.float32)
    coarse = (FINE * np.arange(COARSE)[:, None] * f % LENGTH) * (2.0 * math.pi / LENGTH)
    coarse = np.stack([np.cos(coarse), np.sin(coarse)], axis=1).astype(np.float32)
    coarse = np.broadcast_to(coarse[..., None], (COARSE, 2, FREQS, 128)).copy()
    pick = np.zeros((TAPS, 128), np.float32)
    pick[np.arange(TAPS), 128 - TAPS + np.arange(TAPS)] = 1.0
    return table, np.ascontiguousarray(table.T), band.astype(jnp.bfloat16), fine, coarse, pick.astype(jnp.bfloat16)


def power_kernel(x_ref, pick_ref, s_ref, t_ref):
    ones = jnp.ones((NCHAN, HERE), bf16)
    for w in range(2):
        x = x_ref[w]
        xf = x.astype(f32)
        s_ref[:, w, :] = split_dot(ones, xf * xf, NT)
        t_ref[w] = dot(pick_ref[...], x[:, HERE - 128:], NT).astype(bf16)


def power_and_tail(raw, pick):
    step = 512
    channels = raw.shape[1]
    return pl.pallas_call(
        power_kernel,
        grid=(channels // step,),
        in_specs=[
            pl.BlockSpec((2, step, HERE), lambda i: (0, i, 0)),
            pl.BlockSpec((TAPS, 128), lambda i: (0, 0)),
        ],
        out_specs=[
            pl.BlockSpec((NCHAN, 2, step), lambda i: (0, 0, i)),
            pl.BlockSpec((2, TAPS, step), lambda i: (0, 0, i)),
        ],
        out_shape=[
            jax.ShapeDtypeStruct((NCHAN, 2, channels), f32),
            jax.ShapeDtypeStruct((2, TAPS, channels), bf16),
        ],
        compiler_params=params(),
        cost_estimate=cost(4e8, 5e6),
        name="power",
    )(raw, pick)


def bands(taps, offsets):
    pos = jnp.arange(-TAPS, HERE, dtype=jnp.int32)[:, None]
    out = jnp.arange(OUT, dtype=jnp.int32)[None, :]
    distance = (DECIM * out - pos)[None] + offsets[:, None, None]
    ids = jnp.arange(TAPS, dtype=jnp.int32)[:, None, None, None]
    full = jnp.sum(
        jnp.where(distance[None] == ids, taps.astype(f32)[:, None, None, None], 0.0), axis=0
    ).astype(bf16)
    return full[:, TAPS:], full[:, :TAPS]


def decimate_rows(x, sums, tail, own, prior):
    n = x.shape[0]
    inv = lax.rsqrt(jnp.sum(sums, axis=0, keepdims=True) * (1.0 / SAMPLES) + epsilon)
    cols = jnp.transpose(jnp.broadcast_to(inv, (128, n)))
    cols = jnp.concatenate([cols] * (HERE // 128), axis=1)
    normed = jnp.clip(x.astype(f32) * cols, -clip_level, clip_level).astype(bf16)
    tail_normed = jnp.clip(tail.astype(f32) * inv, -clip_level, clip_level).astype(bf16)
    return (dot(normed, own) + dot(tail_normed, prior, TN)).astype(bf16)


def receive_kernel(x_ref, s_ref, t_ref, own_ref, prior_ref, o_ref):
    for w in range(2):
        o_ref[0, w] = decimate_rows(x_ref[w], s_ref[:, w, :], t_ref[w], own_ref[w], prior_ref[w])


def decimate_receivers(raw, sums, tail, own, prior):
    return pl.pallas_call(
        receive_kernel,
        grid=(NCHAN,),
        in_specs=[
            pl.BlockSpec((2, RECV, HERE), lambda i: (0, i, 0)),
            pl.BlockSpec((NCHAN, 2, RECV), lambda i: (0, 0, i)),
            pl.BlockSpec((2, TAPS, RECV), lambda i: (0, 0, i)),
            pl.BlockSpec((2, HERE, OUT), lambda i: (0, 0, 0)),
            pl.BlockSpec((2, TAPS, OUT), lambda i: (0, 0, 0)),
        ],
        out_specs=pl.BlockSpec((1, 2, RECV, OUT), lambda i: (i, 0, 0, 0)),
        out_shape=jax.ShapeDtypeStruct((NCHAN, 2, RECV, OUT), bf16),
        compiler_params=params(),
        cost_estimate=cost(6e8, 6e6),
        name="decimate_receivers",
    )(raw, sums, tail, own, prior)


def source_kernel(ids_ref, core_ref, x_ref, s_ref, t_ref, own_ref, prior_ref, o_ref):
    first = core_ref[0] == 0
    for w in range(2):
        dec = decimate_rows(x_ref[w], s_ref[:, w, :], t_ref[w], own_ref[w], prior_ref[w])
        for t in range(2):
            for s in range(STAGES):
                low = 64 * t + PART * s
                even, odd = dec[low:low + PART], dec[low + 32:low + 32 + PART]
                o_ref[0, s, w, t] = jnp.where(first, even, odd)
                o_ref[1, s, w, t] = jnp.where(first, odd, even)


def decimate_sources(ids, core, raw, sums, tail, own, prior):
    return pl.pallas_call(
        source_kernel,
        grid_spec=pltpu.PrefetchScalarGridSpec(
            num_scalar_prefetch=2,
            grid=(NSRC,),
            in_specs=[
                pl.BlockSpec((2, 128, HERE), lambda q, ids, c: (0, ids[q], 0)),
                pl.BlockSpec((NCHAN, 2, 128), lambda q, ids, c: (0, 0, ids[q])),
                pl.BlockSpec((2, TAPS, 128), lambda q, ids, c: (0, 0, ids[q])),
                pl.BlockSpec((2, HERE, OUT), lambda q, ids, c: (0, 0, 0)),
                pl.BlockSpec((2, TAPS, OUT), lambda q, ids, c: (0, 0, 0)),
            ],
            out_specs=pl.BlockSpec(
                (2, STAGES, 2, 2, PART, OUT), lambda q, ids, c: (0, 0, 0, q, 0, 0)
            ),
        ),
        out_shape=jax.ShapeDtypeStruct((2, STAGES, 2, NPAIR, PART, OUT), bf16),
        compiler_params=params(),
        cost_estimate=cost(1.5e8, 2e6),
        name="decimate_sources",
    )(ids, core, raw, sums, tail, own, prior)


def receiver_kernel(x_ref, table_ref, o_ref):
    x = jnp.concatenate([x_ref[j, 0] for j in range(NCHAN)], axis=1)
    spec = dot(table_ref[...], x, NT)
    re, im = spec[:FREQS], spec[FREQS:]
    energy = jnp.mean((re * re + im * im).reshape(FREQS // BAND, BAND, RECV), axis=1, keepdims=True)
    gain = lax.rsqrt(energy + epsilon)
    halves = spec.reshape(2, FREQS // BAND, BAND, RECV) * gain[None]
    o_ref[0] = halves.reshape(LENGTH, RECV).astype(bf16)


def receiver_spectra(blocks, table_t):
    return pl.pallas_call(
        receiver_kernel,
        grid=(2,),
        in_specs=[
            pl.BlockSpec((NCHAN, 1, RECV, OUT), lambda w: (0, w, 0, 0)),
            pl.BlockSpec((LENGTH, LENGTH), lambda w: (0, 0)),
        ],
        out_specs=pl.BlockSpec((1, LENGTH, RECV), lambda w: (w, 0, 0)),
        out_shape=jax.ShapeDtypeStruct((2, LENGTH, RECV), bf16),
        compiler_params=params(),
        cost_estimate=cost(1.1e9, 4e6),
        name="receiver_spectra",
    )(blocks, table_t)


def shift_kernel(own_ref, mate_ref, twiddle_ref, o_ref):
    w = pl.program_id(0)
    for c in range(RECV // 128):
        lanes = pl.ds(c * 128, 128)
        spec = jnp.where(w < 2, own_ref[0, :, lanes], mate_ref[0, :, lanes])
        o_ref[:, lanes] = spec
        re, im = spec[:FREQS].astype(f32), spec[FREQS:].astype(f32)
        for a in range(1, COARSE):
            cos, sin = twiddle_ref[a, 0], twiddle_ref[a, 1]
            at = pl.ds(a * RECV + c * 128, 128)
            o_ref[:FREQS, at] = (re * cos + im * sin).astype(bf16)
            o_ref[FREQS:, at] = (im * cos - re * sin).astype(bf16)


def shifted_receivers(own, mate, twiddle):
    return pl.pallas_call(
        shift_kernel,
        grid=(4,),
        in_specs=[
            pl.BlockSpec((1, LENGTH, RECV), lambda w: (jnp.minimum(w, 1), 0, 0)),
            pl.BlockSpec((1, LENGTH, RECV), lambda w: (jnp.maximum(w - 2, 0), 0, 0)),
            pl.BlockSpec((COARSE, 2, FREQS, 128), lambda w: (0, 0, 0, 0)),
        ],
        out_specs=pl.BlockSpec((LENGTH, COARSE * RECV), lambda w: (w, 0)),
        out_shape=jax.ShapeDtypeStruct((4 * LENGTH, COARSE * RECV), bf16),
        compiler_params=params(),
        cost_estimate=cost(3e7, 1.2e7),
        name="shifted_receivers",
    )(own, mate, twiddle)


def correlate_kernel(x_ref, table_ref, band_ref, fine_ref, recv_ref, o_ref, acc_ref):
    w = pl.program_id(0)
    x = jnp.concatenate([x_ref[j, 0] for j in range(NCHAN)], axis=1)
    spec = dot(x, table_ref[...])
    re, im = spec[:, :FREQS], spec[:, FREQS:]
    energy = split_dot(band_ref[...], re * re + im * im, None, flip=True)
    gain = lax.rsqrt(energy + epsilon)
    re = (re * gain).astype(bf16).astype(f32)
    im = (im * gain).astype(bf16).astype(f32)
    cos, sin = fine_ref[:, :FREQS][None], fine_ref[:, FREQS:][None]
    for p in range(NPAIR):
        a = re[p * PART:(p + 1) * PART][:, None, :]
        b = im[p * PART:(p + 1) * PART][:, None, :]
        rows = PART * FINE
        left = jnp.concatenate(
            [
                (a * cos - b * sin).reshape(rows, FREQS).astype(bf16),
                (a * sin + b * cos).reshape(rows, FREQS).astype(bf16),
            ],
            axis=1,
        )
        part = dot(left, recv_ref[...])

        @pl.when(w == 0)
        def _():
            acc_ref[p] = part

        @pl.when((w > 0) & (w < 3))
        def _():
            acc_ref[p] += part

        @pl.when(w == 3)
        def _():
            o_ref[p] = (acc_ref[p] + part).astype(bf16)


def correlate(blocks, table, band, fine, recv):
    rows = PART * FINE
    return pl.pallas_call(
        correlate_kernel,
        grid=(4,),
        in_specs=[
            pl.BlockSpec((NCHAN, 1, ROWS, OUT), lambda w: (0, w, 0, 0)),
            pl.BlockSpec((LENGTH, LENGTH), lambda w: (0, 0)),
            pl.BlockSpec((FREQS, FREQS), lambda w: (0, 0)),
            pl.BlockSpec((FINE, LENGTH), lambda w: (0, 0)),
            pl.BlockSpec((LENGTH, COARSE * RECV), lambda w: (w, 0)),
        ],
        out_specs=pl.BlockSpec((NPAIR, rows, COARSE * RECV), lambda w: (0, 0, 0)),
        out_shape=jax.ShapeDtypeStruct((NPAIR, rows, COARSE * RECV), bf16),
        scratch_shapes=[pltpu.VMEM((NPAIR, rows, COARSE * RECV), f32)],
        compiler_params=params(),
        cost_estimate=cost(2 * 1024 * 1024 * 4096 * 1.2, 1.5e7),
        name="correlate",
    )(blocks, table, band, fine, recv)


def finish_kernel(x_ref, *refs):
    o_ref = refs[-1]
    total = x_ref[0].astype(f32)
    for p in range(1, NPAIR):
        total = total + x_ref[p].astype(f32)
    total = (total * (1.0 / 128.0)).reshape(PART // 2, FINE, COARSE * RECV)
    for a in range(COARSE):
        o_ref[:, a * FINE:(a + 1) * FINE, :] = total[:, :, a * RECV:(a + 1) * RECV]


def finish(parts, stage, out):
    half = PART // 2
    args, specs, aliases = (parts,), [], {}
    if out is not None:
        args, specs, aliases = (parts, out), [pl.BlockSpec(memory_space=pl.ANY)], {1: 0}
    return pl.pallas_call(
        finish_kernel,
        grid=(2,),
        in_specs=[pl.BlockSpec((NPAIR, half * FINE, COARSE * RECV), lambda i: (0, i, 0))] + specs,
        out_specs=pl.BlockSpec((half, 32, RECV), lambda i: (2 * stage + i, 0, 0)),
        out_shape=jax.ShapeDtypeStruct((32, 32, RECV), f32),
        input_output_aliases=aliases,
        compiler_params=params(),
        cost_estimate=cost(1e6, 3e6),
        name="finish",
    )(*args)


def on_device(raw, taps, source_ids, offsets):
    table, table_t, band, fine, coarse, pick = [jnp.asarray(t) for t in tables()]
    core = lax.axis_index("win") % 2
    swap = [(i, i ^ 1) for i in range(2 * NPAIR)]
    groups = [[2 * p + h for p in range(NPAIR)] for h in range(2)]

    sums, tail = power_and_tail(raw, pick)
    sums = lax.all_to_all(sums, "chan", 0, 0, tiled=True)
    tail = lax.ppermute(tail, "chan", [(j, j + 1) for j in range(NCHAN - 1)])
    own, prior = bands(taps, offsets)
    receivers = decimate_receivers(raw, sums, tail, own, prior)
    receivers = lax.all_to_all(receivers, "chan", 0, 0, tiled=True)
    sources = decimate_sources(
        source_ids, core.reshape(1).astype(jnp.int32), raw, sums, tail, own, prior
    )
    mate = lax.ppermute(sources[1], "win", swap)
    both = jnp.concatenate([sources[0], mate], axis=1)
    both = both.reshape(STAGES, 4, ROWS, OUT)
    stages = [
        lax.all_to_all(
            jnp.broadcast_to(both[s][None], (NCHAN, 4, ROWS, OUT)), "chan", 0, 0, tiled=True
        )
        for s in range(STAGES)
    ]
    spectra = receiver_spectra(receivers, table_t)
    recv = shifted_receivers(spectra, lax.ppermute(spectra, "win", swap), coarse)
    out = None
    for s in range(STAGES):
        parts = correlate(stages[s], table, band, fine, recv)
        parts = lax.all_to_all(parts, "win", 0, 0, tiled=True, axis_index_groups=groups)
        out = finish(parts, s, out)
    return out.reshape(1024, RECV)


def solution(mesh):
    placed = (P("win", None, "chan"), P(), P(), P("win"))
    return jax.shard_map(
        on_device, mesh=mesh, in_specs=placed, out_specs=P("win", "chan"), check_vma=False
    )
```

```python
import functools
import math

import jax
import jax.numpy as jnp
import numpy as np
from jax import lax
from jax.experimental import pallas as pl
from jax.experimental.pallas import tpu as pltpu
from jax.sharding import PartitionSpec as P

SAMPLES = 4096
DECIM = 4
TAPS = 32
NSRC = 4
LENGTH = 1024
FREQS = 512
BAND = 64
NCHAN = 8
NPAIR = 8
FINE = 8
COARSE = 4
ORDER = ((1, 1), (0, 3), (1, 2), (1, 3), (0, 1), (0, 2), (1, 0), (0, 0))
WIDTHS = (3, 5)
SPILL = 8
LIMITS = (20, 28)
LOADS = 4
HERE = 512
OUT = HERE // DECIM
RECV = 256

epsilon = 1e-06
clip_level = 2.0

f32 = jnp.float32
bf16 = jnp.bfloat16

NT = (((1,), (1,)), ((), ()))
TN = (((0,), (0,)), ((), ()))


def dot(a, b, dims=None):
    if dims is None:
        return jnp.dot(a, b, preferred_element_type=f32)
    return lax.dot_general(a, b, dims, preferred_element_type=f32)


def split_dot(left, sq, dims, flip=False):
    hi = sq.astype(bf16)
    lo = (sq - hi.astype(f32)).astype(bf16)
    if flip:
        return dot(hi, left, dims) + dot(lo, left, dims)
    return dot(left, hi, dims) + dot(left, lo, dims)


def params(mib):
    return pltpu.CompilerParams(vmem_limit_bytes=mib * 1024 * 1024)


def cost(flops, nbytes):
    return pl.CostEstimate(flops=int(flops), bytes_accessed=int(nbytes), transcendentals=0)


@functools.lru_cache(None)
def tables():
    m = np.arange(LENGTH)[:, None]
    f = np.arange(FREQS)[None, :]
    ang = (m * f % LENGTH).astype(np.float64) * (2.0 * math.pi / LENGTH)
    table = np.concatenate([np.cos(ang), -np.sin(ang)], axis=1).astype(jnp.bfloat16)
    band = np.kron(np.eye(FREQS // BAND), np.ones((BAND, BAND))) / BAND
    lag = np.arange(1, FINE + 1)[:, None]
    fine = (lag * f % LENGTH) * (2.0 * math.pi / LENGTH)
    fine = np.concatenate([np.cos(fine), np.sin(fine)], axis=1).astype(np.float32)
    coarse = (FINE * np.arange(1, COARSE)[:, None] * f % LENGTH) * (2.0 * math.pi / LENGTH)
    coarse = np.stack([np.cos(coarse), np.sin(coarse)], axis=1).astype(np.float32)
    coarse = np.pad(coarse.reshape(2 * COARSE - 2, FREQS).T, ((0, 0), (0, 128 - 2 * COARSE + 2)))
    edge = np.zeros((LENGTH, NCHAN, 2 * SPILL), np.float32)
    for j in range(NCHAN - 1):
        cols = table[OUT * (j + 1):OUT * (j + 1) + SPILL].astype(np.float32).T
        edge[:, j, :SPILL] = cols
    edge = edge.reshape(LENGTH, NCHAN * 2 * SPILL).astype(jnp.bfloat16)
    pick = np.zeros((TAPS, 128), np.float32)
    pick[np.arange(TAPS), 128 - TAPS + np.arange(TAPS)] = 1.0
    flipped = np.ascontiguousarray(table.T)
    return table, flipped, edge, band.astype(jnp.bfloat16), fine, coarse, pick.astype(jnp.bfloat16)


def raw_copies(raw_ref, buf, sems):
    step = buf.shape[1] // LOADS
    copies = []
    for i in range(LOADS):
        rows = pl.ds(i * step, step)
        copies.append(pltpu.make_async_copy(raw_ref.at[:, rows, :], buf.at[:, rows, :], sems.at[i]))
    for copy in copies:
        copy.start()
    return copies, step


def raw_scratch(raw):
    return [pltpu.VMEM(raw.shape, bf16), pltpu.SemaphoreType.DMA((LOADS,))]


def power_kernel(raw_ref, pick_ref, s_ref, t_ref, buf, sems):
    ones = jnp.ones((NCHAN, 128), bf16)
    copies, step = raw_copies(raw_ref, buf, sems)
    for i, copy in enumerate(copies):
        copy.wait()
        rows = pl.ds(i * step, step)
        for w in range(2):
            total = None
            for c in range(0, HERE, 128):
                x = buf[w, rows, c:c + 128].astype(f32)
                total = x * x if total is None else total + x * x
            s_ref[:, w, rows] = split_dot(ones, total, NT)
            t_ref[w, :, rows] = dot(pick_ref[...], buf[w, rows, HERE - 128:], NT).astype(bf16)


def power_and_tail(raw, pick):
    channels = raw.shape[1]
    return pl.pallas_call(
        power_kernel,
        in_specs=[pl.BlockSpec(memory_space=pltpu.HBM), pl.BlockSpec(memory_space=pltpu.VMEM)],
        out_specs=[pl.BlockSpec(memory_space=pltpu.VMEM)] * 2,
        out_shape=[
            jax.ShapeDtypeStruct((NCHAN, 2, channels), f32),
            jax.ShapeDtypeStruct((2, TAPS, channels), bf16),
        ],
        scratch_shapes=raw_scratch(raw),
        compiler_params=params(51),
        cost_estimate=cost(4e8, 5e6),
        name="power",
    )(raw, pick)


def band(taps, offsets, pos, out):
    distance = (DECIM * out - pos)[None] + offsets[:, None, None]
    ids = jnp.arange(TAPS, dtype=jnp.int32)[:, None, None, None]
    return jnp.sum(
        jnp.where(distance[None] == ids, taps.astype(f32)[:, None, None, None], 0.0), axis=0
    ).astype(bf16)


def bands(taps, offsets):
    here = jnp.arange(HERE, dtype=jnp.int32)[:, None]
    before = jnp.arange(-TAPS, 0, dtype=jnp.int32)[:, None]
    back = jnp.arange(-128, 0, dtype=jnp.int32)[None, :]
    out = jnp.arange(OUT, dtype=jnp.int32)[None, :]
    first = jnp.arange(SPILL, dtype=jnp.int32)[:, None]
    return band(taps, offsets, here, out), band(taps, offsets, before, out), band(taps, offsets, back, first)


def normalize(x, sums):
    n = x.shape[0]
    inv = lax.rsqrt(jnp.sum(sums, axis=0, keepdims=True) * (1.0 / SAMPLES) + epsilon)
    cols = jnp.transpose(jnp.broadcast_to(inv, (128, n)))
    cols = jnp.concatenate([cols] * (HERE // 128), axis=1)
    return jnp.clip(x.astype(f32) * cols, -clip_level, clip_level).astype(bf16), inv


def receive_kernel(raw_ref, s_ref, own_ref, spill_ref, o_ref, buf, sems):
    copies, step = raw_copies(raw_ref, buf, sems)
    for i, copy in enumerate(copies):
        copy.wait()
        rows = pl.ds(i * step, step)
        for w in range(2):
            normed, _ = normalize(buf[w, rows, :], s_ref[:, w, rows])
            dec = dot(normed, own_ref[w]).astype(bf16)
            over = dot(spill_ref[w], normed[:, HERE - 128:], NT)
            for j in range(step // RECV):
                at = i * (step // RECV) + j
                o_ref[at, w, :RECV] = dec[j * RECV:(j + 1) * RECV]
                lanes = j * RECV
                o_ref[at, w, RECV:] = jnp.concatenate(
                    [over[:, lanes:lanes + 128], over[:, lanes + 128:lanes + 256]], axis=0
                ).astype(bf16)


def decimate_receivers(raw, sums, own, spill):
    v = pl.BlockSpec(memory_space=pltpu.VMEM)
    return pl.pallas_call(
        receive_kernel,
        in_specs=[pl.BlockSpec(memory_space=pltpu.HBM), v, v, v],
        out_specs=v,
        out_shape=jax.ShapeDtypeStruct((NCHAN, 2, RECV + 2 * SPILL, OUT), bf16),
        scratch_shapes=raw_scratch(raw),
        compiler_params=params(51),
        cost_estimate=cost(6e8, 6e6),
        name="decimate_receivers",
    )(raw, sums, own, spill)


def source_kernel(ids_ref, me_ref, raw_ref, s_ref, t_ref, own_ref, prior_ref, o_ref, buf, sems):
    me = me_ref[0]
    first = me % 2 == 0
    y, x = me // 8, me // 2 % 4
    copies = []
    for q in range(NSRC):
        rows = pl.ds(pl.multiple_of(ids_ref[q] * 128, 128), 128)
        copies.append(pltpu.make_async_copy(raw_ref.at[:, rows, :], buf.at[q], sems.at[q]))
    for copy in copies:
        copy.start()
    for q in range(NSRC):
        copies[q].wait()
        lanes = pl.ds(pl.multiple_of(ids_ref[q] * 128, 128), 128)
        for w in range(2):
            normed, inv = normalize(buf[q, w], s_ref[:, w, lanes])
            tail = jnp.clip(t_ref[w, :, lanes].astype(f32) * inv, -clip_level, clip_level).astype(bf16)
            dec = (dot(normed, own_ref[w]) + dot(tail, prior_ref[w], TN)).astype(bf16)
            for t in range(2):
                pair = 2 * q + t
                away = (pair // 4 - y) % 2 * 4 + (pair % 4 - x) % 4
                at = sum(jnp.where(away == 4 * dy + dx, k, 0) for k, (dy, dx) in enumerate(ORDER))
                even, odd = dec[64 * t:64 * t + 32], dec[64 * t + 32:64 * t + 64]
                o_ref[0, w, at] = jnp.where(first, even, odd)
                o_ref[1, w, at] = jnp.where(first, odd, even)


def decimate_sources(ids, me, raw, sums, tail, own, prior):
    v = pl.BlockSpec(memory_space=pltpu.VMEM)
    smem = pl.BlockSpec(memory_space=pltpu.SMEM)
    return pl.pallas_call(
        source_kernel,
        in_specs=[smem, smem, pl.BlockSpec(memory_space=pltpu.HBM), v, v, v, v],
        out_specs=v,
        out_shape=jax.ShapeDtypeStruct((2, 2, NPAIR, 32, OUT), bf16),
        scratch_shapes=[pltpu.VMEM((NSRC, 2, 128, HERE), bf16), pltpu.SemaphoreType.DMA((NSRC,))],
        compiler_params=params(51),
        cost_estimate=cost(1.5e8, 2e6),
        name="decimate_sources",
    )(ids, me, raw, sums, tail, own, prior)


def receiver_kernel(x_ref, table_ref, edge_ref, twiddle_ref, o_ref):
    x = jnp.concatenate([x_ref[j, 0, :RECV] for j in range(NCHAN)], axis=1)
    over = jnp.concatenate([x_ref[j, 0, RECV:] for j in range(NCHAN)], axis=0)
    spec = dot(table_ref[...], x, NT)
    over = over.astype(f32)
    turned = jnp.concatenate([over[SPILL:], over[:SPILL]], axis=0)
    spec = spec + dot(edge_ref[...], jnp.concatenate([over, turned], axis=1).astype(bf16))
    re, im = spec[:FREQS], spec[FREQS:]
    energy = jnp.mean((re * re + im * im).reshape(FREQS // BAND, BAND, RECV), axis=1, keepdims=True)
    gain = lax.rsqrt(energy + epsilon)
    re = (re.reshape(FREQS // BAND, BAND, RECV) * gain).reshape(FREQS, RECV).astype(bf16)
    im = (im.reshape(FREQS // BAND, BAND, RECV) * gain).reshape(FREQS, RECV).astype(bf16)
    o_ref[:FREQS, :RECV] = re
    o_ref[FREQS:, :RECV] = im
    re, im = re.astype(f32), im.astype(f32)
    for a in range(1, COARSE):
        cos = jnp.broadcast_to(twiddle_ref[:, 2 * a - 2:2 * a - 1], (FREQS, 128))
        sin = jnp.broadcast_to(twiddle_ref[:, 2 * a - 1:2 * a], (FREQS, 128))
        for c in range(0, RECV, 128):
            p, q = re[:, c:c + 128], im[:, c:c + 128]
            at = pl.ds(a * RECV + c, 128)
            o_ref[:FREQS, at] = (p * cos + q * sin).astype(bf16)
            o_ref[FREQS:, at] = (q * cos - p * sin).astype(bf16)


def shifted_receivers(x, table_t, edge, twiddle):
    return pl.pallas_call(
        receiver_kernel,
        grid=(2,),
        in_specs=[
            pl.BlockSpec((NCHAN, 1, RECV + 2 * SPILL, OUT), lambda w: (0, w, 0, 0)),
            pl.BlockSpec(table_t.shape, lambda w: (0, 0)),
            pl.BlockSpec(edge.shape, lambda w: (0, 0)),
            pl.BlockSpec(twiddle.shape, lambda w: (0, 0)),
        ],
        out_specs=pl.BlockSpec((LENGTH, COARSE * RECV), lambda w: (w, 0)),
        out_shape=jax.ShapeDtypeStruct((2 * LENGTH, COARSE * RECV), bf16),
        compiler_params=params(LIMITS[0]),
        cost_estimate=cost(1e7, 1e4),
        name="shifted_receivers",
    )(x, table_t, edge, twiddle)


def correlate_kernel(count, me_ref, x0, x1, x2, x3, table_ref, band_ref, fine_ref, early_ref, late_ref, *refs):
    outs, (x_ref, s_ref, l0_ref, l1_ref) = refs[:count], refs[count:]
    part = 32 * count
    me = me_ref[1]
    z, y = me // 2, me % 2
    for dz, x in enumerate((x0, x1, x2, x3)):
        for dy in range(2):
            block = (z - dz) % 4 * 2 + (y + dy) % 2
            lanes = pl.ds(pl.multiple_of(block * OUT, OUT), OUT)
            for core in range(2):
                rows = pl.ds(core * 2 * part, 2 * part)
                x_ref[rows, lanes] = x[2 * dy + core].reshape(2 * part, OUT)
    spec = dot(x_ref[...], table_ref[...])
    re, im = spec[:, :FREQS], spec[:, FREQS:]
    gain = lax.rsqrt(split_dot(band_ref[...], re * re + im * im, None, flip=True) + epsilon)
    s_ref[:, :, :FREQS] = (re * gain).astype(bf16).reshape(4, part, FREQS)
    s_ref[:, :, FREQS:] = (im * gain).astype(bf16).reshape(4, part, FREQS)
    rows = 16 * FINE
    for k, o_ref in enumerate(outs):
        left_ref = (l0_ref, l1_ref)[k % 2]
        for w in range(4):
            for f in range(0, FREQS, 128):
                cos = fine_ref[:, f:f + 128][None]
                sin = fine_ref[:, FREQS + f:FREQS + f + 128][None]
                for c in range(0, 32, 16):
                    a = s_ref[w, 32 * k + c:32 * k + c + 16, f:f + 128].astype(f32)[:, None, :]
                    b = s_ref[w, 32 * k + c:32 * k + c + 16, FREQS + f:FREQS + f + 128].astype(f32)[:, None, :]
                    at = w * LENGTH + f
                    here = pl.ds(c * FINE, rows)
                    left_ref[here, at:at + 128] = (a * cos - b * sin).reshape(rows, 128).astype(bf16)
                    left_ref[here, at + FREQS:at + FREQS + 128] = (a * sin + b * cos).reshape(rows, 128).astype(bf16)
        total = dot(left_ref[:, :2 * LENGTH], early_ref[...])
        total = total + dot(left_ref[:, 2 * LENGTH:], late_ref[...])
        o_ref[...] = total.astype(o_ref.dtype)


def correlate(me, blocks, table, band, fine, early, late, last):
    count = blocks[0].shape[2] // 32
    rows = 32 * FINE
    v = pl.BlockSpec(memory_space=pltpu.VMEM)
    shape = (rows, COARSE * RECV)
    kinds = [bf16] * (count - 1) + [f32 if last else bf16]
    return pl.pallas_call(
        functools.partial(correlate_kernel, count),
        in_specs=[pl.BlockSpec(memory_space=pltpu.SMEM)] + [v] * 9,
        out_specs=[v] * count,
        out_shape=[jax.ShapeDtypeStruct(shape, kind) for kind in kinds],
        scratch_shapes=[
            pltpu.VMEM((4 * 32 * count, LENGTH), bf16),
            pltpu.VMEM((4, 32 * count, LENGTH), bf16),
            pltpu.VMEM((rows, 4 * LENGTH), bf16),
            pltpu.VMEM((rows, 4 * LENGTH), bf16),
        ],
        compiler_params=params(LIMITS[1]),
        cost_estimate=cost(2.5e9 * count, 4e6),
        name="correlate",
    )(me, *blocks, table, band, fine, early, late)


def presum_kernel(*refs):
    total = refs[0][...].astype(f32)
    for ref in refs[1:-1]:
        total = total + ref[...].astype(f32)
    refs[-1][...] = total


def presum(parts):
    shape = parts[0].shape
    half = shape[0] // 2
    return pl.pallas_call(
        presum_kernel,
        grid=(2,),
        in_specs=[pl.BlockSpec((half, shape[1]), lambda i: (i, 0))] * len(parts),
        out_specs=pl.BlockSpec((half, shape[1]), lambda i: (i, 0)),
        out_shape=jax.ShapeDtypeStruct(shape, f32),
        compiler_params=params(16),
        cost_estimate=cost(1e6, 3e6),
        name="presum",
    )(*parts)


def finish_kernel(*refs):
    o_ref = refs[-1]
    total = refs[0][...].astype(f32)
    for ref in refs[1:-1]:
        total = total + ref[...].astype(f32)
    total = (total * (1.0 / 128.0)).reshape(16, FINE, COARSE * RECV)
    for a in range(COARSE):
        o_ref[:, a * FINE:(a + 1) * FINE, :] = total[:, :, a * RECV:(a + 1) * RECV]


def finish(parts):
    shape = parts[0].shape
    half = shape[0] // 2
    return pl.pallas_call(
        finish_kernel,
        grid=(2,),
        in_specs=[pl.BlockSpec((half, shape[1]), lambda i: (i, 0))] * len(parts),
        out_specs=pl.BlockSpec((16, 32, RECV), lambda i: (i, 0, 0)),
        out_shape=jax.ShapeDtypeStruct((32, 32, RECV), f32),
        compiler_params=params(16),
        cost_estimate=cost(1e6, 3e6),
        name="finish",
    )(*parts)


def gather_pairs(sources):
    mine, other = sources[0], sources[1]
    axes = ("chan", "win")
    ways = []
    for dy in range(2):
        for core in range(2):
            piece = other if core else mine
            if dy or core:
                route = [
                    (16 * j + i, 16 * (j ^ dy) + (i ^ core))
                    for j in range(NCHAN) for i in range(2 * NPAIR)
                ]
                piece = lax.ppermute(piece, axes, route)
            ways.append(piece)
    packs, at = [], 0
    for wide in WIDTHS:
        packs.append(jnp.stack([p[:, at:at + wide].reshape(2, wide * 32, OUT) for p in ways]))
        at += wide
    return packs


def spread(pack, dz):
    return lax.ppermute(pack, "chan", [(j, (j + 2 * dz) % NCHAN) for j in range(NCHAN)])


def on_device(raw, taps, source_ids, offsets):
    table, table_t, edge, ones, fine, coarse, pick = [jnp.asarray(t) for t in tables()]
    me = jnp.stack([lax.axis_index("win"), lax.axis_index("chan")]).astype(jnp.int32)
    swap = [(i, i ^ 1) for i in range(2 * NPAIR)]

    sums, tail = power_and_tail(raw, pick)
    sums = lax.all_to_all(sums, "chan", 0, 0, tiled=True)
    tail = lax.ppermute(tail, "chan", [(j, j + 1) for j in range(NCHAN - 1)])
    own, prior, spill = bands(taps, offsets)
    receivers = decimate_receivers(raw, sums, own, spill)
    receivers, tail = lax.optimization_barrier((receivers, tail))
    receivers = lax.all_to_all(receivers, "chan", 0, 0, tiled=True)
    sources = decimate_sources(source_ids, me, raw, sums, tail, own, prior)
    packs = gather_pairs(sources)
    receivers, *packs = lax.optimization_barrier((receivers, *packs))
    early = shifted_receivers(receivers, table_t, edge, coarse)
    early, packs[1] = lax.optimization_barrier((early, packs[1]))
    late = shifted_receivers(lax.ppermute(receivers, "win", swap), table_t, edge, coarse)
    stages = [[pack] + [spread(pack, dz) for dz in (1, 2, 3)] for pack in packs]
    arrived = []
    for blocks in stages:
        made = correlate(me, blocks, table, ones, fine, early, late, blocks is stages[-1])
        for piece in made:
            dy, dx = ORDER[len(arrived)]
            if (dy, dx) != (0, 0):
                route = [
                    (8 * y + 2 * x + c, 8 * ((y + dy) % 2) + 2 * ((x + dx) % 4) + c)
                    for y in range(2) for x in range(4) for c in range(2)
                ]
                piece = lax.ppermute(piece, "win", route)
            arrived.append(piece)
    early = presum(arrived[:3])
    return finish([early] + arrived[3:]).reshape(1024, RECV)


def solution(mesh):
    placed = (P("win", None, "chan"), P(), P(), P("win"))
    return jax.shard_map(
        on_device, mesh=mesh, in_specs=placed, out_specs=P("win", "chan"), check_vma=False
    )
```

```python
import functools
import math

import jax
import jax.numpy as jnp
import numpy as np
from jax import lax
from jax.experimental import pallas as pl
from jax.experimental.pallas import tpu as pltpu
from jax.sharding import PartitionSpec as P

SAMPLES = 4096
DECIM = 4
TAPS = 32
NSRC = 4
LENGTH = 1024
FREQS = 512
BAND = 64
NCHAN = 8
NPAIR = 8
FINE = 8
COARSE = 4
GROUPS = (
    (1, 0, 0), (1, 1, 0), (1, 2, 0), (1, 3, 0), (0, 2, 1), (1, 2, 1),
    (0, 1, 1), (1, 1, 1), (0, 3, 1), (1, 3, 1),
    (0, 1, 0), (0, 2, 0), (0, 3, 0), (0, 0, 0), (0, 0, 1), (1, 0, 1),
)
WIDTHS = (3, 5)
SIZES = tuple(2 * 32 * n + 32 for n in WIDTHS)
SPILL_ROWS = (SIZES[0] - 32, SIZES[0] + SIZES[1] - 32)
ROW_OF = tuple(
    tuple(
        32 * (w * WIDTHS[0] + k) if k < WIDTHS[0] else SIZES[0] + 32 * (w * WIDTHS[1] + k - WIDTHS[0])
        for k in range(NPAIR)
    )
    for w in range(2)
)
SPILL = 8
LIMITS = (20, 28)
LOADS = 4
HERE = 512
OUT = HERE // DECIM
RECV = 256

epsilon = 1e-06
clip_level = 2.0

f32 = jnp.float32
bf16 = jnp.bfloat16

NT = (((1,), (1,)), ((), ()))
TN = (((0,), (0,)), ((), ()))


def dot(a, b, dims=None):
    if dims is None:
        return jnp.dot(a, b, preferred_element_type=f32)
    return lax.dot_general(a, b, dims, preferred_element_type=f32)


def split_dot(left, sq, dims, flip=False):
    hi = sq.astype(bf16)
    lo = (sq - hi.astype(f32)).astype(bf16)
    if flip:
        return dot(hi, left, dims) + dot(lo, left, dims)
    return dot(left, hi, dims) + dot(left, lo, dims)


def params(mib):
    return pltpu.CompilerParams(vmem_limit_bytes=mib * 1024 * 1024)


def cost(flops, nbytes):
    return pl.CostEstimate(flops=int(flops), bytes_accessed=int(nbytes), transcendentals=0)


@functools.lru_cache(None)
def tables():
    m = np.arange(LENGTH)[:, None]
    f = np.arange(FREQS)[None, :]
    ang = (m * f % LENGTH).astype(np.float64) * (2.0 * math.pi / LENGTH)
    table = np.concatenate([np.cos(ang), -np.sin(ang)], axis=1).astype(jnp.bfloat16)
    band = np.kron(np.eye(FREQS // BAND), np.ones((BAND, BAND))) / BAND
    lag = np.arange(1, FINE + 1)[:, None]
    fine = (lag * f % LENGTH) * (2.0 * math.pi / LENGTH)
    fine = np.concatenate([np.cos(fine), np.sin(fine)], axis=1).astype(np.float32)
    coarse = (FINE * np.arange(1, COARSE)[:, None] * f % LENGTH) * (2.0 * math.pi / LENGTH)
    coarse = np.stack([np.cos(coarse), np.sin(coarse)], axis=1).astype(np.float32)
    coarse = np.pad(coarse.reshape(2 * COARSE - 2, FREQS).T, ((0, 0), (0, 128 - 2 * COARSE + 2)))
    edge = np.zeros((LENGTH, NCHAN, 2 * SPILL), np.float32)
    for j in range(NCHAN - 1):
        cols = table[OUT * (j + 1):OUT * (j + 1) + SPILL].astype(np.float32).T
        edge[:, j, :SPILL] = cols
    edge = edge.reshape(LENGTH, NCHAN * 2 * SPILL).astype(jnp.bfloat16)
    flipped = np.ascontiguousarray(table.T)
    return table, flipped, edge, band.astype(jnp.bfloat16), fine, coarse


def raw_copies(raw_ref, buf, sems):
    step = buf.shape[1] // LOADS
    copies = []
    for i in range(LOADS):
        rows = pl.ds(i * step, step)
        copies.append(pltpu.make_async_copy(raw_ref.at[:, rows, :], buf.at[:, rows, :], sems.at[i]))
    for copy in copies:
        copy.start()
    return copies, step


def raw_scratch(raw):
    return [pltpu.VMEM(raw.shape, bf16), pltpu.SemaphoreType.DMA((LOADS,))]


def power_kernel(raw_ref, s_ref, buf, sems):
    ones = jnp.ones((NCHAN, 128), bf16)
    copies, step = raw_copies(raw_ref, buf, sems)
    for i, copy in enumerate(copies):
        copy.wait()
        rows = pl.ds(i * step, step)
        for w in range(2):
            total = None
            for c in range(0, HERE, 128):
                x = buf[w, rows, c:c + 128].astype(f32)
                total = x * x if total is None else total + x * x
            s_ref[:, w, rows] = split_dot(ones, total, NT)


def power(raw):
    return pl.pallas_call(
        power_kernel,
        in_specs=[pl.BlockSpec(memory_space=pltpu.HBM)],
        out_specs=pl.BlockSpec(memory_space=pltpu.VMEM),
        out_shape=jax.ShapeDtypeStruct((NCHAN, 2, raw.shape[1]), f32),
        scratch_shapes=raw_scratch(raw),
        compiler_params=params(53),
        cost_estimate=cost(4e8, 5e6),
        name="power",
    )(raw)


def band(taps, offsets, pos, out):
    distance = (DECIM * out - pos)[None] + offsets[:, None, None]
    ids = jnp.arange(TAPS, dtype=jnp.int32)[:, None, None, None]
    return jnp.sum(
        jnp.where(distance[None] == ids, taps.astype(f32)[:, None, None, None], 0.0), axis=0
    ).astype(bf16)


def bands(taps, offsets):
    here = jnp.arange(HERE, dtype=jnp.int32)[:, None]
    back = jnp.arange(-128, 0, dtype=jnp.int32)
    out = jnp.arange(OUT, dtype=jnp.int32)[None, :]
    first = jnp.arange(SPILL, dtype=jnp.int32)[:, None]
    edge = jnp.where(out < SPILL, out, HERE)
    return (
        band(taps, offsets, here, out),
        band(taps, offsets, back[None, :], first),
        band(taps, offsets, back[:, None], edge),
    )


def normalize(x, sums):
    n = x.shape[0]
    inv = lax.rsqrt(jnp.sum(sums, axis=0, keepdims=True) * (1.0 / SAMPLES) + epsilon)
    cols = jnp.transpose(jnp.broadcast_to(inv, (128, n)))
    cols = jnp.concatenate([cols] * (HERE // 128), axis=1)
    return jnp.clip(x.astype(f32) * cols, -clip_level, clip_level).astype(bf16)


def decimate_kernel(
    ids_ref, me_ref, raw_ref, s_ref, own_ref, spill_ref, edge_ref, recv_ref, mine_ref, other_ref, buf, sems
):
    copies, step = raw_copies(raw_ref, buf, sems)
    for i, copy in enumerate(copies):
        copy.wait()
        rows = pl.ds(i * step, step)
        for w in range(2):
            normed = normalize(buf[w, rows, :], s_ref[:, w, rows])
            dec = dot(normed, own_ref[w]).astype(bf16)
            over = dot(spill_ref[w], normed[:, HERE - 128:], NT)
            for j in range(step // RECV):
                at = i * (step // RECV) + j
                recv_ref[at, w, :RECV] = dec[j * RECV:(j + 1) * RECV]
                lanes = j * RECV
                recv_ref[at, w, RECV:] = jnp.concatenate(
                    [over[:, lanes:lanes + 128], over[:, lanes + 128:lanes + 256]], axis=0
                ).astype(bf16)
    me = me_ref[0]
    first = me % 2 == 0
    y, x = me // 8, me // 2 % 4
    spills = [[jnp.zeros((16, 128), f32)] * 2 for _ in range(2)]
    for q in range(NSRC):
        here = pl.ds(pl.multiple_of(ids_ref[q] * 128, 128), 128)
        for w in range(2):
            normed = normalize(buf[w, here, :], s_ref[:, w, here])
            dec = dot(normed, own_ref[w])
            over = dot(normed[:, HERE - 128:], edge_ref[w])
            for t in range(2):
                pair = 2 * q + t
                away = (pair // 4 - y) % 2 * 4 + (pair % 4 - x) % 4
                for half in range(2):
                    at = sum(
                        jnp.where(away == 4 * dy + dx, g, 0)
                        for g, (dy, dx, which) in enumerate(GROUPS) if which == half
                    )
                    unit, odd = at // 2, at % 2
                    row = sum(jnp.where(unit == k, ROW_OF[w][k], 0) for k in range(NPAIR)) + 16 * odd
                    rows = pl.ds(pl.multiple_of(row, 16), 16)
                    low = 64 * t + 16 * half
                    for side, out_ref in enumerate((mine_ref, other_ref)):
                        pick = first if side == 0 else jnp.logical_not(first)
                        out_ref[rows, :] = jnp.where(
                            pick, dec[low:low + 16], dec[low + 32:low + 48]
                        ).astype(bf16)
                        turned = jnp.where(pick, over[low:low + 16], over[low + 32:low + 48])
                        turned = pltpu.roll(turned, 8 * (NPAIR * w + unit), 1)
                        for par in range(2):
                            spills[side][par] = spills[side][par] + jnp.where(odd == par, turned, 0.0)
    for spill, out_ref in zip(spills, (mine_ref, other_ref)):
        for low in SPILL_ROWS:
            out_ref[low:low + 32, :] = jnp.concatenate(spill, axis=0).astype(bf16)


def decimate(ids, me, raw, sums, own, spill, edge):
    v = pl.BlockSpec(memory_space=pltpu.VMEM)
    smem = pl.BlockSpec(memory_space=pltpu.SMEM)
    return pl.pallas_call(
        decimate_kernel,
        in_specs=[smem, smem, pl.BlockSpec(memory_space=pltpu.HBM), v, v, v, v],
        out_specs=[v, v, v],
        out_shape=[
            jax.ShapeDtypeStruct((NCHAN, 2, RECV + 2 * SPILL, OUT), bf16),
            jax.ShapeDtypeStruct((sum(SIZES), OUT), bf16),
            jax.ShapeDtypeStruct((sum(SIZES), OUT), bf16),
        ],
        scratch_shapes=raw_scratch(raw),
        compiler_params=params(53),
        cost_estimate=cost(6e8, 6e6),
        name="decimate",
    )(ids, me, raw, sums, own, spill, edge)


def pack_kernel(mine_ref, other_ref, *outs):
    at = 0
    for size, out_ref in zip(SIZES, outs):
        out_ref[0] = mine_ref[at:at + size]
        out_ref[1] = other_ref[at:at + size]
        at += size


def pack(mine, other):
    v = pl.BlockSpec(memory_space=pltpu.VMEM)
    return pl.pallas_call(
        pack_kernel,
        in_specs=[v, v],
        out_specs=[v] * len(SIZES),
        out_shape=[jax.ShapeDtypeStruct((2, size, OUT), bf16) for size in SIZES],
        compiler_params=params(8),
        cost_estimate=cost(1e4, 1e4),
        name="pack",
    )(mine, other)


def stack_kernel(*refs):
    for i, ref in enumerate(refs[:-1]):
        refs[-1][i] = ref[...]


def stack(parts):
    v = pl.BlockSpec(memory_space=pltpu.VMEM)
    return pl.pallas_call(
        stack_kernel,
        in_specs=[v] * len(parts),
        out_specs=v,
        out_shape=jax.ShapeDtypeStruct((len(parts),) + parts[0].shape, bf16),
        compiler_params=params(8),
        cost_estimate=cost(1e4, 1e4),
        name="stack",
    )(*parts)


def receiver_kernel(x_ref, table_ref, edge_ref, twiddle_ref, o_ref):
    x = jnp.concatenate([x_ref[j, 0, :RECV] for j in range(NCHAN)], axis=1)
    over = jnp.concatenate([x_ref[j, 0, RECV:] for j in range(NCHAN)], axis=0)
    spec = dot(table_ref[...], x, NT)
    over = over.astype(f32)
    turned = jnp.concatenate([over[SPILL:], over[:SPILL]], axis=0)
    spec = spec + dot(edge_ref[...], jnp.concatenate([over, turned], axis=1).astype(bf16))
    re, im = spec[:FREQS], spec[FREQS:]
    energy = jnp.mean((re * re + im * im).reshape(FREQS // BAND, BAND, RECV), axis=1, keepdims=True)
    gain = lax.rsqrt(energy + epsilon)
    re = (re.reshape(FREQS // BAND, BAND, RECV) * gain).reshape(FREQS, RECV).astype(bf16)
    im = (im.reshape(FREQS // BAND, BAND, RECV) * gain).reshape(FREQS, RECV).astype(bf16)
    o_ref[:FREQS, :RECV] = re
    o_ref[FREQS:, :RECV] = im
    re, im = re.astype(f32), im.astype(f32)
    for a in range(1, COARSE):
        cos = jnp.broadcast_to(twiddle_ref[:, 2 * a - 2:2 * a - 1], (FREQS, 128))
        sin = jnp.broadcast_to(twiddle_ref[:, 2 * a - 1:2 * a], (FREQS, 128))
        for c in range(0, RECV, 128):
            p, q = re[:, c:c + 128], im[:, c:c + 128]
            at = pl.ds(a * RECV + c, 128)
            o_ref[:FREQS, at] = (p * cos + q * sin).astype(bf16)
            o_ref[FREQS:, at] = (q * cos - p * sin).astype(bf16)


def shifted_receivers(x, table_t, edge, twiddle, flops):
    return pl.pallas_call(
        receiver_kernel,
        grid=(2,),
        in_specs=[
            pl.BlockSpec((NCHAN, 1, RECV + 2 * SPILL, OUT), lambda w: (0, w, 0, 0)),
            pl.BlockSpec(table_t.shape, lambda w: (0, 0)),
            pl.BlockSpec(edge.shape, lambda w: (0, 0)),
            pl.BlockSpec(twiddle.shape, lambda w: (0, 0)),
        ],
        out_specs=pl.BlockSpec((LENGTH, COARSE * RECV), lambda w: (w, 0)),
        out_shape=jax.ShapeDtypeStruct((2 * LENGTH, COARSE * RECV), bf16),
        compiler_params=params(LIMITS[0]),
        cost_estimate=cost(flops, 1e4),
        name="shifted_receivers",
    )(x, table_t, edge, twiddle)


def correlate_kernel(stage, first, count, widths, me_ref, *refs):
    parts = 2 if stage == 0 else 4
    srcs = refs[:parts]
    table_ref, band_ref, fine_ref, early_ref, late_ref = refs[parts:parts + 5]
    outs = refs[parts + 5:parts + 5 + len(widths)]
    x_ref, s_ref, l0_ref, l1_ref = refs[parts + 5 + len(widths):]
    part = 32 * count
    wide = 32 * WIDTHS[stage]
    me = me_ref[1]
    z, y = me // 2, me % 2
    pieces = []
    for dz in range(4):
        for dy in range(2):
            block = (z - dz) % 4 * 2 + (y + dy) % 2
            for core in range(2):
                src = srcs[dy].at[dz, core] if stage == 0 else srcs[dz].at[dy, core]
                pieces.append((src, block, core * 2 * part))
    for src, block, low in pieces:
        lanes = pl.ds(pl.multiple_of(block * OUT, OUT), OUT)
        for w in range(2):
            x_ref[low + w * part:low + (w + 1) * part, lanes] = src[w * wide + 32 * first:w * wide + 32 * first + part]
    lane = lax.broadcasted_iota(jnp.int32, (32, OUT), 1)
    for src, block, low in pieces:
        lanes = pl.ds(pl.multiple_of((block + 1) * OUT, OUT), OUT)
        spill = src[2 * wide:2 * wide + 32].astype(f32)
        for w in range(2):
            for k in range(count):
                group = NPAIR * w + sum(WIDTHS[:stage]) + first + k
                turned = jnp.where(lane < SPILL, pltpu.roll(spill, (128 - 8 * group) % 128, 1), 0.0)
                rows = slice(low + w * part + 32 * k, low + w * part + 32 * k + 32)
                x_ref[rows, lanes] = (x_ref[rows, lanes].astype(f32) + turned).astype(bf16)
    spec = dot(x_ref[:, :LENGTH], table_ref[...])
    re, im = spec[:, :FREQS], spec[:, FREQS:]
    gain = lax.rsqrt(split_dot(band_ref[...], re * re + im * im, None, flip=True) + epsilon)
    s_ref[:, :, :FREQS] = (re * gain).astype(bf16).reshape(4, part, FREQS)
    s_ref[:, :, FREQS:] = (im * gain).astype(bf16).reshape(4, part, FREQS)
    rows = 16 * FINE
    places = [(out, i) for out, n in zip(outs, widths) for i in range(n)]
    for k, (o_ref, place) in enumerate(places):
        left_ref = (l0_ref, l1_ref)[k % 2]
        for w in range(4):
            for f in range(0, FREQS, 128):
                cos = fine_ref[:, f:f + 128][None]
                sin = fine_ref[:, FREQS + f:FREQS + f + 128][None]
                for c in range(0, 32, 16):
                    a = s_ref[w, 32 * k + c:32 * k + c + 16, f:f + 128].astype(f32)[:, None, :]
                    b = s_ref[w, 32 * k + c:32 * k + c + 16, FREQS + f:FREQS + f + 128].astype(f32)[:, None, :]
                    at = w * LENGTH + f
                    here = pl.ds(c * FINE, rows)
                    left_ref[here, at:at + 128] = (a * cos - b * sin).reshape(rows, 128).astype(bf16)
                    left_ref[here, at + FREQS:at + FREQS + 128] = (a * sin + b * cos).reshape(rows, 128).astype(bf16)
        total = dot(left_ref[:, :2 * LENGTH], early_ref[...])
        total = total + dot(left_ref[:, 2 * LENGTH:], late_ref[...])
        o_ref[place * 2 * rows:(place + 1) * 2 * rows] = total.astype(o_ref.dtype)


def correlate(me, parts, stage, first, widths, kind, table, band, fine, early, late):
    count = sum(widths)
    rows = 32 * FINE
    v = pl.BlockSpec(memory_space=pltpu.VMEM)
    return pl.pallas_call(
        functools.partial(correlate_kernel, stage, first, count, widths),
        in_specs=[pl.BlockSpec(memory_space=pltpu.SMEM)] + [v] * (len(parts) + 5),
        out_specs=[v] * len(widths),
        out_shape=[jax.ShapeDtypeStruct((n * rows, COARSE * RECV), kind) for n in widths],
        scratch_shapes=[
            pltpu.VMEM((4 * 32 * count, LENGTH + OUT), bf16),
            pltpu.VMEM((4, 32 * count, LENGTH), bf16),
            pltpu.VMEM((rows, 4 * LENGTH), bf16),
            pltpu.VMEM((rows, 4 * LENGTH), bf16),
        ],
        compiler_params=params(LIMITS[1]),
        cost_estimate=cost(2.5e9 * count, 4e6),
        name="correlate",
    )(me, *parts, table, band, fine, early, late)


def local(kernel, args, shapes, name):
    v = pl.BlockSpec(memory_space=pltpu.VMEM)
    return pl.pallas_call(
        kernel,
        in_specs=[v] * len(args),
        out_specs=[v] * len(shapes),
        out_shape=shapes,
        compiler_params=params(16),
        cost_estimate=cost(1e6, 2e6),
        name=name,
    )(*args)


def merge_kernel(own_ref, got_ref, o1_ref, o2_ref, o3_ref, keep_ref):
    n = keep_ref.shape[0]
    for i, out_ref in enumerate((o1_ref, o2_ref, o3_ref, keep_ref)):
        at = (i + 1) % 4 * n
        total = own_ref[i * n:(i + 1) * n] + got_ref[at:at + n].astype(f32)
        out_ref[...] = total.astype(out_ref.dtype)


def merge(own, got):
    n = own.shape[0] // 4
    shape = (n, own.shape[1])
    kinds = (bf16, bf16, bf16, f32)
    return local(merge_kernel, (own, got), [jax.ShapeDtypeStruct(shape, k) for k in kinds], "merge")


def cross_kernel(own_ref, *refs):
    n = refs[-1].shape[0]
    total = own_ref[n:]
    for ref in refs[:-1]:
        total = total + ref[n:].astype(f32)
    refs[-1][...] = total.astype(bf16)


def cross(own, got):
    shape = jax.ShapeDtypeStruct((own.shape[0] // 2, own.shape[1]), bf16)
    return local(cross_kernel, (own, *got), [shape], "cross")[0]


def finish_kernel(own_ref, b1_ref, b2_ref, b3_ref, far_ref, keep_ref, a1_ref, a2_ref, a3_ref, o_ref):
    n = keep_ref.shape[0]
    low = keep_ref[...]
    for ref in (a1_ref, a2_ref, a3_ref):
        low = low + ref[...].astype(f32)
    high = own_ref[:n] + far_ref[...].astype(f32)
    for ref in (b1_ref, b2_ref, b3_ref):
        high = high + ref[:n].astype(f32)
    for i, total in enumerate((low, high)):
        total = (total * (1.0 / 128.0)).reshape(16, FINE, COARSE * RECV)
        for a in range(COARSE):
            o_ref[16 * i:16 * i + 16, a * FINE:(a + 1) * FINE, :] = total[:, :, a * RECV:(a + 1) * RECV]


def finish(own, got, far, keep, moved):
    shape = jax.ShapeDtypeStruct((32, 32, RECV), f32)
    return local(finish_kernel, (own, *got, far, keep, *moved), [shape], "finish")[0]


def route(dy, dx):
    return [
        (8 * y + 2 * x + c, 8 * ((y + dy) % 2) + 2 * ((x + dx) % 4) + c)
        for y in range(2) for x in range(4) for c in range(2)
    ]


def send(piece, dy, dx):
    return lax.ppermute(piece, "win", route(dy, dx))


def spread(part, dz, dy):
    way = [(j, (j // 2 + dz) % 4 * 2 + (j + dy) % 2) for j in range(NCHAN)]
    return lax.ppermute(part, "chan", way) if dz or dy else part


def on_device(raw, taps, source_ids, offsets):
    table, table_t, edge, ones, fine, coarse = [jnp.asarray(t) for t in tables()]
    me = jnp.stack([lax.axis_index("win"), lax.axis_index("chan")]).astype(jnp.int32)
    swap = [(i, i ^ 1) for i in range(2 * NPAIR)]

    sums = lax.all_to_all(power(raw), "chan", 0, 0, tiled=True)
    receivers, mine, other = decimate(source_ids, me, raw, sums, *bands(taps, offsets))
    receivers = lax.all_to_all(receivers, "chan", 0, 0, tiled=True)
    packs = pack(mine, lax.ppermute(other, "win", swap))
    around = [spread(packs[0], dz, 0) for dz in range(4)]
    receivers = lax.optimization_barrier((receivers, *packs))[0]
    early = shifted_receivers(receivers, table_t, edge, coarse, 1e10)
    early, *around = lax.optimization_barrier((early, *around))
    near = stack(around)
    both = stack((packs[1], spread(packs[1], 0, 1)))
    mate = lax.optimization_barrier((lax.ppermute(receivers, "win", swap), early, near, both))[0]
    near = (near, spread(near, 0, 1))
    late = shifted_receivers(mate, table_t, edge, coarse, 1e10)
    late, both = lax.optimization_barrier((late, both))
    rest = [spread(both, dz, 0) for dz in range(4)]
    shared = (table, ones, fine, early, late)
    y_low, x2 = correlate(me, near, 0, 0, (2, 1), bf16, *shared)
    y_low, x2 = send(y_low, 1, 0), send(x2, 0, 2)
    x1, x3 = correlate(me, rest, 1, 0, (1, 1), bf16, *shared)
    x1, x3 = send(x1, 0, 1), send(x3, 0, 3)
    own_low, own_high = correlate(me, rest, 1, 2, (2, 1), f32, *shared)
    *moved, keep = merge(own_low, y_low)
    moved = [send(piece, 0, dx) for dx, piece in zip((1, 2, 3), moved)]
    far = send(cross(own_high, (x2, x1, x3)), 1, 0)
    return finish(own_high, (x2, x1, x3), far, keep, moved).reshape(1024, RECV)


def solution(mesh):
    placed = (P("win", None, "chan"), P(), P(), P("win"))
    return jax.shard_map(
        on_device, mesh=mesh, in_specs=placed, out_specs=P("win", "chan"), check_vma=False
    )
```

```python
import functools
import math

import jax
import jax.numpy as jnp
import numpy as np
from jax import lax
from jax.experimental import pallas as pl
from jax.experimental.pallas import tpu as pltpu
from jax.sharding import PartitionSpec as P

SAMPLES = 4096
DECIM = 4
TAPS = 32
NSRC = 4
LENGTH = 1024
FREQS = 512
BAND = 64
NCHAN = 8
NPAIR = 8
FINE = 8
COARSE = 4
GROUPS = (
    (1, 1, 0), (1, 2, 0), (1, 3, 0), (1, 0, 0), (0, 2, 1), (1, 2, 1),
    (0, 1, 1), (1, 1, 1), (0, 3, 1), (1, 3, 1),
    (0, 1, 0), (0, 2, 0), (0, 3, 0), (0, 0, 0), (0, 0, 1), (1, 0, 1),
)
WIDTHS = (3, 5)
SIZES = tuple(2 * 32 * n + 32 for n in WIDTHS)
SPILL_ROWS = (SIZES[0] - 32, SIZES[0] + SIZES[1] - 32)
ROW_OF = tuple(
    tuple(
        32 * (w * WIDTHS[0] + k) if k < WIDTHS[0] else SIZES[0] + 32 * (w * WIDTHS[1] + k - WIDTHS[0])
        for k in range(NPAIR)
    )
    for w in range(2)
)
SPILL = 8
LIMITS = (20, 28)
LOADS = 4
HERE = 512
OUT = HERE // DECIM
RECV = 256

epsilon = 1e-06
clip_level = 2.0

f32 = jnp.float32
bf16 = jnp.bfloat16

NT = (((1,), (1,)), ((), ()))
TN = (((0,), (0,)), ((), ()))


def dot(a, b, dims=None):
    if dims is None:
        return jnp.dot(a, b, preferred_element_type=f32)
    return lax.dot_general(a, b, dims, preferred_element_type=f32)


def split_dot(left, sq, dims, flip=False):
    hi = sq.astype(bf16)
    lo = (sq - hi.astype(f32)).astype(bf16)
    if flip:
        return dot(hi, left, dims) + dot(lo, left, dims)
    return dot(left, hi, dims) + dot(left, lo, dims)


def params(mib):
    return pltpu.CompilerParams(vmem_limit_bytes=mib * 1024 * 1024)


def cost(flops, nbytes):
    return pl.CostEstimate(flops=int(flops), bytes_accessed=int(nbytes), transcendentals=0)


@functools.lru_cache(None)
def tables():
    m = np.arange(LENGTH)[:, None]
    f = np.arange(FREQS)[None, :]
    ang = (m * f % LENGTH).astype(np.float64) * (2.0 * math.pi / LENGTH)
    table = np.concatenate([np.cos(ang), -np.sin(ang)], axis=1).astype(jnp.bfloat16)
    band = np.kron(np.eye(FREQS // BAND), np.ones((BAND, BAND))) / BAND
    lag = np.arange(1, FINE + 1)[:, None]
    fine = (lag * f % LENGTH) * (2.0 * math.pi / LENGTH)
    fine = np.concatenate([np.cos(fine), np.sin(fine)], axis=1).astype(np.float32)
    coarse = (FINE * np.arange(1, COARSE)[:, None] * f % LENGTH) * (2.0 * math.pi / LENGTH)
    coarse = np.stack([np.cos(coarse), np.sin(coarse)], axis=1).astype(np.float32)
    coarse = np.pad(coarse.reshape(2 * COARSE - 2, FREQS).T, ((0, 0), (0, 128 - 2 * COARSE + 2)))
    edge = np.zeros((LENGTH, NCHAN, 2 * SPILL), np.float32)
    for j in range(NCHAN - 1):
        cols = table[OUT * (j + 1):OUT * (j + 1) + SPILL].astype(np.float32).T
        edge[:, j, :SPILL] = cols
    edge = edge.reshape(LENGTH, NCHAN * 2 * SPILL).astype(jnp.bfloat16)
    flipped = np.ascontiguousarray(table.T)
    return table, flipped, edge, band.astype(jnp.bfloat16), fine, coarse


def raw_copies(raw_ref, buf, sems):
    step = buf.shape[1] // LOADS
    copies = []
    for i in range(LOADS):
        rows = pl.ds(i * step, step)
        copies.append(pltpu.make_async_copy(raw_ref.at[:, rows, :], buf.at[:, rows, :], sems.at[i]))
    for copy in copies:
        copy.start()
    return copies, step


def raw_scratch(raw):
    return [pltpu.VMEM(raw.shape, bf16), pltpu.SemaphoreType.DMA((LOADS,))]


def power_kernel(raw_ref, s_ref, buf, sems):
    ones = jnp.ones((NCHAN, 128), bf16)
    copies, step = raw_copies(raw_ref, buf, sems)
    for i, copy in enumerate(copies):
        copy.wait()
        rows = pl.ds(i * step, step)
        for w in range(2):
            total = None
            for c in range(0, HERE, 128):
                x = buf[w, rows, c:c + 128].astype(f32)
                total = x * x if total is None else total + x * x
            s_ref[:, w, rows] = split_dot(ones, total, NT)


def power(raw):
    return pl.pallas_call(
        power_kernel,
        in_specs=[pl.BlockSpec(memory_space=pltpu.HBM)],
        out_specs=pl.BlockSpec(memory_space=pltpu.VMEM),
        out_shape=jax.ShapeDtypeStruct((NCHAN, 2, raw.shape[1]), f32),
        scratch_shapes=raw_scratch(raw),
        compiler_params=params(53),
        cost_estimate=cost(4e8, 5e6),
        name="power",
    )(raw)


def band(taps, offsets, pos, out):
    distance = (DECIM * out - pos)[None] + offsets[:, None, None]
    ids = jnp.arange(TAPS, dtype=jnp.int32)[:, None, None, None]
    return jnp.sum(
        jnp.where(distance[None] == ids, taps.astype(f32)[:, None, None, None], 0.0), axis=0
    ).astype(bf16)


def bands(taps, offsets):
    here = jnp.arange(HERE, dtype=jnp.int32)[:, None]
    back = jnp.arange(-128, 0, dtype=jnp.int32)
    out = jnp.arange(OUT, dtype=jnp.int32)[None, :]
    first = jnp.arange(SPILL, dtype=jnp.int32)[:, None]
    edge = jnp.where(out < SPILL, out, HERE)
    return (
        band(taps, offsets, here, out),
        band(taps, offsets, back[None, :], first),
        band(taps, offsets, back[:, None], edge),
    )


def normalize(x, sums):
    n = x.shape[0]
    inv = lax.rsqrt(jnp.sum(sums, axis=0, keepdims=True) * (1.0 / SAMPLES) + epsilon)
    cols = jnp.transpose(jnp.broadcast_to(inv, (128, n)))
    cols = jnp.concatenate([cols] * (HERE // 128), axis=1)
    return jnp.clip(x.astype(f32) * cols, -clip_level, clip_level).astype(bf16)


def decimate_kernel(
    ids_ref, me_ref, raw_ref, s_ref, own_ref, spill_ref, edge_ref, recv_ref, mine_ref, other_ref, buf, sems
):
    copies, step = raw_copies(raw_ref, buf, sems)
    for i, copy in enumerate(copies):
        copy.wait()
        rows = pl.ds(i * step, step)
        for w in range(2):
            normed = normalize(buf[w, rows, :], s_ref[:, w, rows])
            dec = dot(normed, own_ref[w]).astype(bf16)
            over = dot(spill_ref[w], normed[:, HERE - 128:], NT)
            for j in range(step // RECV):
                at = i * (step // RECV) + j
                recv_ref[at, w, :RECV] = dec[j * RECV:(j + 1) * RECV]
                lanes = j * RECV
                recv_ref[at, w, RECV:] = jnp.concatenate(
                    [over[:, lanes:lanes + 128], over[:, lanes + 128:lanes + 256]], axis=0
                ).astype(bf16)
    me = me_ref[0]
    first = me % 2 == 0
    y, x = me // 8, me // 2 % 4
    spills = [[jnp.zeros((16, 128), f32)] * 2 for _ in range(2)]
    for q in range(NSRC):
        here = pl.ds(pl.multiple_of(ids_ref[q] * 128, 128), 128)
        for w in range(2):
            normed = normalize(buf[w, here, :], s_ref[:, w, here])
            dec = dot(normed, own_ref[w])
            over = dot(normed[:, HERE - 128:], edge_ref[w])
            for t in range(2):
                pair = 2 * q + t
                away = (pair // 4 - y) % 2 * 4 + (pair % 4 - x) % 4
                for half in range(2):
                    at = sum(
                        jnp.where(away == 4 * dy + dx, g, 0)
                        for g, (dy, dx, which) in enumerate(GROUPS) if which == half
                    )
                    unit, odd = at // 2, at % 2
                    row = sum(jnp.where(unit == k, ROW_OF[w][k], 0) for k in range(NPAIR)) + 16 * odd
                    rows = pl.ds(pl.multiple_of(row, 16), 16)
                    low = 64 * t + 16 * half
                    for side, out_ref in enumerate((mine_ref, other_ref)):
                        pick = first if side == 0 else jnp.logical_not(first)
                        out_ref[rows, :] = jnp.where(
                            pick, dec[low:low + 16], dec[low + 32:low + 48]
                        ).astype(bf16)
                        turned = jnp.where(pick, over[low:low + 16], over[low + 32:low + 48])
                        turned = pltpu.roll(turned, 8 * (NPAIR * w + unit), 1)
                        for par in range(2):
                            spills[side][par] = spills[side][par] + jnp.where(odd == par, turned, 0.0)
    for spill, out_ref in zip(spills, (mine_ref, other_ref)):
        for low in SPILL_ROWS:
            out_ref[low:low + 32, :] = jnp.concatenate(spill, axis=0).astype(bf16)


def decimate(ids, me, raw, sums, own, spill, edge):
    v = pl.BlockSpec(memory_space=pltpu.VMEM)
    smem = pl.BlockSpec(memory_space=pltpu.SMEM)
    return pl.pallas_call(
        decimate_kernel,
        in_specs=[smem, smem, pl.BlockSpec(memory_space=pltpu.HBM), v, v, v, v],
        out_specs=[v, v, v],
        out_shape=[
            jax.ShapeDtypeStruct((NCHAN, 2, RECV + 2 * SPILL, OUT), bf16),
            jax.ShapeDtypeStruct((sum(SIZES), OUT), bf16),
            jax.ShapeDtypeStruct((sum(SIZES), OUT), bf16),
        ],
        scratch_shapes=raw_scratch(raw),
        compiler_params=params(53),
        cost_estimate=cost(6e8, 6e6),
        name="decimate",
    )(ids, me, raw, sums, own, spill, edge)


def pack_kernel(mine_ref, other_ref, *outs):
    at = 0
    for size, out_ref in zip(SIZES, outs):
        out_ref[0] = mine_ref[at:at + size]
        out_ref[1] = other_ref[at:at + size]
        at += size


def pack(mine, other):
    v = pl.BlockSpec(memory_space=pltpu.VMEM)
    return pl.pallas_call(
        pack_kernel,
        in_specs=[v, v],
        out_specs=[v] * len(SIZES),
        out_shape=[jax.ShapeDtypeStruct((2, size, OUT), bf16) for size in SIZES],
        compiler_params=params(8),
        cost_estimate=cost(1e4, 1e4),
        name="pack",
    )(mine, other)


def stack_kernel(*refs):
    for i, ref in enumerate(refs[:-1]):
        refs[-1][i] = ref[...]


def stack(parts, limit=8):
    v = pl.BlockSpec(memory_space=pltpu.VMEM)
    return pl.pallas_call(
        stack_kernel,
        in_specs=[v] * len(parts),
        out_specs=v,
        out_shape=jax.ShapeDtypeStruct((len(parts),) + parts[0].shape, bf16),
        compiler_params=params(limit),
        cost_estimate=cost(1e4, 1e4),
        name="stack",
    )(*parts)


def receiver_kernel(x_ref, table_ref, edge_ref, twiddle_ref, o_ref):
    x = jnp.concatenate([x_ref[j, 0, :RECV] for j in range(NCHAN)], axis=1)
    over = jnp.concatenate([x_ref[j, 0, RECV:] for j in range(NCHAN)], axis=0)
    spec = dot(table_ref[...], x, NT)
    over = over.astype(f32)
    turned = jnp.concatenate([over[SPILL:], over[:SPILL]], axis=0)
    spec = spec + dot(edge_ref[...], jnp.concatenate([over, turned], axis=1).astype(bf16))
    re, im = spec[:FREQS], spec[FREQS:]
    energy = jnp.mean((re * re + im * im).reshape(FREQS // BAND, BAND, RECV), axis=1, keepdims=True)
    gain = lax.rsqrt(energy + epsilon)
    re = (re.reshape(FREQS // BAND, BAND, RECV) * gain).reshape(FREQS, RECV).astype(bf16)
    im = (im.reshape(FREQS // BAND, BAND, RECV) * gain).reshape(FREQS, RECV).astype(bf16)
    o_ref[:FREQS, :RECV] = re
    o_ref[FREQS:, :RECV] = im
    re, im = re.astype(f32), im.astype(f32)
    for a in range(1, COARSE):
        cos = jnp.broadcast_to(twiddle_ref[:, 2 * a - 2:2 * a - 1], (FREQS, 128))
        sin = jnp.broadcast_to(twiddle_ref[:, 2 * a - 1:2 * a], (FREQS, 128))
        for c in range(0, RECV, 128):
            p, q = re[:, c:c + 128], im[:, c:c + 128]
            at = pl.ds(a * RECV + c, 128)
            o_ref[:FREQS, at] = (p * cos + q * sin).astype(bf16)
            o_ref[FREQS:, at] = (q * cos - p * sin).astype(bf16)


def shifted_receivers(x, table_t, edge, twiddle, flops):
    return pl.pallas_call(
        receiver_kernel,
        grid=(2,),
        in_specs=[
            pl.BlockSpec((NCHAN, 1, RECV + 2 * SPILL, OUT), lambda w: (0, w, 0, 0)),
            pl.BlockSpec(table_t.shape, lambda w: (0, 0)),
            pl.BlockSpec(edge.shape, lambda w: (0, 0)),
            pl.BlockSpec(twiddle.shape, lambda w: (0, 0)),
        ],
        out_specs=pl.BlockSpec((LENGTH, COARSE * RECV), lambda w: (w, 0)),
        out_shape=jax.ShapeDtypeStruct((2 * LENGTH, COARSE * RECV), bf16),
        compiler_params=params(LIMITS[0]),
        cost_estimate=cost(flops, 1e4),
        name="shifted_receivers",
    )(x, table_t, edge, twiddle)


def correlate_kernel(stage, first, count, widths, me_ref, *refs):
    parts = 2 if stage == 0 else 4
    srcs = refs[:parts]
    table_ref, band_ref, fine_ref, early_ref, late_ref = refs[parts:parts + 5]
    outs = refs[parts + 5:parts + 5 + len(widths)]
    x_ref, s_ref, l0_ref, l1_ref = refs[parts + 5 + len(widths):]
    part = 32 * count
    wide = 32 * WIDTHS[stage]
    me = me_ref[1]
    z, y = me // 2, me % 2
    pieces = []
    for dz in range(4):
        for dy in range(2):
            block = (z - dz) % 4 * 2 + (y + dy) % 2
            for core in range(2):
                src = srcs[dy].at[dz, core] if stage == 0 else srcs[dz].at[dy, core]
                pieces.append((src, block, core * 2 * part))
    for src, block, low in pieces:
        lanes = pl.ds(pl.multiple_of(block * OUT, OUT), OUT)
        for w in range(2):
            x_ref[low + w * part:low + (w + 1) * part, lanes] = src[w * wide + 32 * first:w * wide + 32 * first + part]
    lane = lax.broadcasted_iota(jnp.int32, (32, OUT), 1)
    for src, block, low in pieces:
        lanes = pl.ds(pl.multiple_of((block + 1) * OUT, OUT), OUT)
        spill = src[2 * wide:2 * wide + 32].astype(f32)
        for w in range(2):
            for k in range(count):
                group = NPAIR * w + sum(WIDTHS[:stage]) + first + k
                turned = jnp.where(lane < SPILL, pltpu.roll(spill, (128 - 8 * group) % 128, 1), 0.0)
                rows = slice(low + w * part + 32 * k, low + w * part + 32 * k + 32)
                x_ref[rows, lanes] = (x_ref[rows, lanes].astype(f32) + turned).astype(bf16)
    spec = dot(x_ref[:, :LENGTH], table_ref[...])
    re, im = spec[:, :FREQS], spec[:, FREQS:]
    gain = lax.rsqrt(split_dot(band_ref[...], re * re + im * im, None, flip=True) + epsilon)
    s_ref[:, :, :FREQS] = (re * gain).astype(bf16).reshape(4, part, FREQS)
    s_ref[:, :, FREQS:] = (im * gain).astype(bf16).reshape(4, part, FREQS)
    rows = 16 * FINE
    places = [(out, i) for out, n in zip(outs, widths) for i in range(n)]
    for k, (o_ref, place) in enumerate(places):
        left_ref = (l0_ref, l1_ref)[k % 2]
        for w in range(4):
            for f in range(0, FREQS, 128):
                cos = fine_ref[:, f:f + 128][None]
                sin = fine_ref[:, FREQS + f:FREQS + f + 128][None]
                for c in range(0, 32, 16):
                    a = s_ref[w, 32 * k + c:32 * k + c + 16, f:f + 128].astype(f32)[:, None, :]
                    b = s_ref[w, 32 * k + c:32 * k + c + 16, FREQS + f:FREQS + f + 128].astype(f32)[:, None, :]
                    at = w * LENGTH + f
                    here = pl.ds(c * FINE, rows)
                    left_ref[here, at:at + 128] = (a * cos - b * sin).reshape(rows, 128).astype(bf16)
                    left_ref[here, at + FREQS:at + FREQS + 128] = (a * sin + b * cos).reshape(rows, 128).astype(bf16)
        total = dot(left_ref[:, :2 * LENGTH], early_ref[...])
        total = total + dot(left_ref[:, 2 * LENGTH:], late_ref[...])
        o_ref[place * 2 * rows:(place + 1) * 2 * rows] = total.astype(o_ref.dtype)


def correlate(me, parts, stage, first, widths, kind, table, band, fine, early, late):
    count = sum(widths)
    rows = 32 * FINE
    v = pl.BlockSpec(memory_space=pltpu.VMEM)
    return pl.pallas_call(
        functools.partial(correlate_kernel, stage, first, count, widths),
        in_specs=[pl.BlockSpec(memory_space=pltpu.SMEM)] + [v] * (len(parts) + 5),
        out_specs=[v] * len(widths),
        out_shape=[jax.ShapeDtypeStruct((n * rows, COARSE * RECV), kind) for n in widths],
        scratch_shapes=[
            pltpu.VMEM((4 * 32 * count, LENGTH + OUT), bf16),
            pltpu.VMEM((4, 32 * count, LENGTH), bf16),
            pltpu.VMEM((rows, 4 * LENGTH), bf16),
            pltpu.VMEM((rows, 4 * LENGTH), bf16),
        ],
        compiler_params=params(LIMITS[1]),
        cost_estimate=cost(2.5e9 * count, 4e6),
        name="correlate",
    )(me, *parts, table, band, fine, early, late)


def local(kernel, args, shapes, name):
    v = pl.BlockSpec(memory_space=pltpu.VMEM)
    return pl.pallas_call(
        kernel,
        in_specs=[v] * len(args),
        out_specs=[v] * len(shapes),
        out_shape=shapes,
        compiler_params=params(16),
        cost_estimate=cost(1e6, 2e6),
        name=name,
    )(*args)


def merge_kernel(own_ref, got_ref, o0_ref, o1_ref):
    n = o0_ref.shape[0]
    for i, out_ref in enumerate((o0_ref, o1_ref)):
        total = own_ref[i * n:(i + 1) * n] + got_ref[i * n:(i + 1) * n].astype(f32)
        out_ref[...] = total.astype(out_ref.dtype)


def merge(own, got, kinds):
    shape = (own.shape[0] // 2, own.shape[1])
    return local(merge_kernel, (own, got), [jax.ShapeDtypeStruct(shape, k) for k in kinds], "merge")


def cross_kernel(own_ref, *refs):
    n = refs[-1].shape[0]
    total = own_ref[n:]
    for ref in refs[:-1]:
        total = total + ref[n:].astype(f32)
    refs[-1][...] = total.astype(bf16)


def cross(own, got):
    shape = jax.ShapeDtypeStruct((own.shape[0] // 2, own.shape[1]), bf16)
    return local(cross_kernel, (own, *got), [shape], "cross")[0]


def finish_kernel(own_ref, b1_ref, b2_ref, b3_ref, far_ref, keep_ref, a1_ref, a2_ref, a3_ref, o_ref):
    n = keep_ref.shape[0]
    low = keep_ref[...]
    for ref in (a1_ref, a2_ref, a3_ref):
        low = low + ref[...].astype(f32)
    high = own_ref[:n] + far_ref[...].astype(f32)
    for ref in (b1_ref, b2_ref, b3_ref):
        high = high + ref[:n].astype(f32)
    for i, total in enumerate((low, high)):
        total = (total * (1.0 / 128.0)).reshape(16, FINE, COARSE * RECV)
        for a in range(COARSE):
            o_ref[16 * i:16 * i + 16, a * FINE:(a + 1) * FINE, :] = total[:, :, a * RECV:(a + 1) * RECV]


def finish(own, got, far, keep, moved):
    shape = jax.ShapeDtypeStruct((32, 32, RECV), f32)
    return local(finish_kernel, (own, *got, far, keep, *moved), [shape], "finish")[0]


def route(dy, dx):
    return [
        (8 * y + 2 * x + c, 8 * ((y + dy) % 2) + 2 * ((x + dx) % 4) + c)
        for y in range(2) for x in range(4) for c in range(2)
    ]


def send(piece, dy, dx):
    return lax.ppermute(piece, "win", route(dy, dx))


def spread(part, dz, dy):
    way = [(j, (j // 2 + dz) % 4 * 2 + (j + dy) % 2) for j in range(NCHAN)]
    return lax.ppermute(part, "chan", way) if dz or dy else part


def on_device(raw, taps, source_ids, offsets):
    table, table_t, edge, ones, fine, coarse = [jnp.asarray(t) for t in tables()]
    me = jnp.stack([lax.axis_index("win"), lax.axis_index("chan")]).astype(jnp.int32)
    swap = [(i, i ^ 1) for i in range(2 * NPAIR)]

    sums = lax.all_to_all(power(raw), "chan", 0, 0, tiled=True)
    receivers, mine, other = decimate(source_ids, me, raw, sums, *bands(taps, offsets))
    receivers = lax.all_to_all(receivers, "chan", 0, 0, tiled=True)
    packs = list(pack(mine, lax.ppermute(other, "win", swap)))
    around = [spread(packs[0], dz, 0) for dz in range(4)]
    across = spread(packs[1], 0, 1)
    receivers, packs[1], *around = lax.optimization_barrier((receivers, packs[1], *around))
    near = stack(around, 53)
    receivers, near = lax.optimization_barrier((receivers, near))
    early = shifted_receivers(receivers, table_t, edge, coarse, 1e10)
    both = stack((packs[1], across))
    mate = lax.optimization_barrier((lax.ppermute(receivers, "win", swap), early, near, both))[0]
    near = (near, spread(near, 0, 1))
    late = shifted_receivers(mate, table_t, edge, coarse, 1e10)
    late, both = lax.optimization_barrier((late, both))
    rest = [spread(both, dz, 0) for dz in range(4)]
    shared = (table, ones, fine, early, late)
    y_one, y_two, x2 = correlate(me, near, 0, 0, (1, 1, 1), bf16, *shared)
    y_one, y_two, x2 = send(y_one, 1, 0), send(y_two, 1, 0), send(x2, 0, 2)
    x1, x3 = correlate(me, rest, 1, 0, (1, 1), bf16, *shared)
    x1, x3 = send(x1, 0, 1), send(x3, 0, 3)
    own_one = correlate(me, rest, 1, 2, (1,), f32, *shared)[0]
    a1, a2 = merge(own_one, y_one, (bf16, bf16))
    a1, a2, me = lax.optimization_barrier((a1, a2, me))
    a1, a2 = send(a1, 0, 1), send(a2, 0, 2)
    own_two, own_high = correlate(me, rest, 1, 3, (1, 1), f32, *shared)
    a3, keep = merge(own_two, y_two, (bf16, f32))
    a3 = send(a3, 0, 3)
    far = send(cross(own_high, (x2, x1, x3)), 1, 0)
    return finish(own_high, (x2, x1, x3), far, keep, (a1, a2, a3)).reshape(1024, RECV)


def solution(mesh):
    placed = (P("win", None, "chan"), P(), P(), P("win"))
    return jax.shard_map(
        on_device, mesh=mesh, in_specs=placed, out_specs=P("win", "chan"), check_vma=False
    )
```
